32 devices in a mesh: seq: 2 (over y), pos: 16 (over z, x, core).
Axes of the slice: x: 2, y: 2, z: 4, core: 2. Of those that a mesh axis runs over, the one named last changes fastest.
Arguments:
- states: int32 [256, 256], P('seq', 'pos'), may hold values from 0 to 20
- multiplicity: int32 [256], P('seq'), may hold values from 1 to 8
- fields: float32 [256, 21], P('pos'), may hold values from -3 to 360
- diag_couplings: float32 [16, 336, 336], P('pos'), may hold values from -12 to 12
- slot_couplings: float32 [16, 4, 336, 336], P('pos'), may hold values from -12 to 12
- slot_blocks: int32 [16, 4], replicated, may hold values from -1 to 15, as said below
- partner_blocks: int32 [16, 4], replicated, may hold values from -1 to 15, as said below
Outputs:
- new_fields: float32 [256, 21], P('pos')
- new_diag: float32 [16, 336, 336], P('pos')
- new_slots: float32 [16, 4, 336, 336], P('pos')
The draws below stay inside these ranges and needn't reach their ends.
Inputs may be any that keep to these rules, and one draw needn't show every extreme that they name: slot_blocks[c, t] is the block whose conditionals use the couplings in slot t of block c, or -1 for an empty slot. Slot 0 holds c - 1 and slot 1 holds c + 1 where such a block exists; the other slots hold blocks at least two away from c; no block stands twice in one row or in one column. partner_blocks[b] lists candidate partner blocks of block b, or -1: entry 0 is b - 1 and entry 1 is b + 1 where they exist; entry t >= 2 is -1 or the block c with slot_blocks[c, t] = b.
All inputs are finite; a program needn't handle non-finite values.
Results may differ from the reference program's by a relative error of at most 0.0025.
Values may be sent and summed in bfloat16 or wider, within the bound.
A program may use at most 64 MiB of HBM per device.

```python
import math
import jax
import jax.numpy as jnp
from jax import lax

Q = 21
BLK = 16
SLOTS = 4
K = 336
NB = 16
L = 256
NSEQ = 256


def pair_tables(key):
    base_key = jax.random.fold_in(key, 1009)
    block_ids = jnp.arange(NB, dtype=jnp.int32)
    absent = jnp.full((NB,), -1, jnp.int32)
    below_block = jnp.where(block_ids >= 1, block_ids - 1, absent)
    above_block = jnp.where(block_ids <= NB - 2, block_ids + 1, absent)
    owner_cols = [below_block, above_block]
    lister_cols = [below_block, above_block]
    chosen = []
    for column in range(SLOTS - 2):
        slot_key = jax.random.fold_in(base_key, column)
        shuffled = jax.random.permutation(jax.random.fold_in(slot_key, 1), NB).astype(jnp.int32)
        active = jax.random.randint(jax.random.fold_in(slot_key, 2), (NB,), 0, 4) > 0
        usable = active & (jnp.abs(shuffled - block_ids) >= 2)
        for earlier in chosen:
            usable = usable & (shuffled != earlier)
        held = jnp.where(usable, shuffled, absent)
        chosen.append(held)
        owner_cols.append(held)
        inverse = jnp.zeros((NB,), jnp.int32).at[shuffled].set(block_ids)
        kept = jax.random.randint(jax.random.fold_in(slot_key, 3), (NB,), 0, 4) > 0
        lister_cols.append(jnp.where(usable[inverse] & kept, inverse, absent))
    return (jnp.stack(owner_cols, axis=1), jnp.stack(lister_cols, axis=1))


def draw_slot_blocks(key, part):
    return pair_tables(key)[0]


def draw_partner_blocks(key, part):
    return pair_tables(key)[1]


def coupling_values(key, leading):
    subkeys = jax.random.split(key, 4)
    entries = jnp.clip(jax.random.normal(subkeys[0], leading + (BLK, Q, BLK, Q), jnp.float32), -4.0, 4.0)
    groups = jnp.exp(jax.random.uniform(subkeys[1], leading + (BLK, 1, BLK, 1), jnp.float32, math.log(0.1), 0.0))
    row_scale = jnp.exp(jax.random.uniform(subkeys[2], leading + (BLK, Q, 1, 1), jnp.float32, 0.0, math.log(10.0)))
    col_scale = jnp.exp(jax.random.uniform(subkeys[3], leading + (1, 1, BLK, Q), jnp.float32, 0.0, math.log(10.0)))
    values = 0.03 * entries * groups * row_scale * col_scale
    return values.reshape(leading + (BLK * Q, BLK * Q))


def draw_diag_couplings(key, part):
    return coupling_values(jax.random.fold_in(key, 3), (NB,))


def draw_slot_couplings(key, part):
    return coupling_values(jax.random.fold_in(key, 5), (NB, SLOTS))


def draw_fields(key, part):
    subkeys = jax.random.split(key, 1)
    return jnp.clip(0.7 * jax.random.normal(subkeys[0], (L, Q), jnp.float32), -3.0, 3.0)


def set_ends(values, own_key, smallest, high):
    longest = values.shape.index(max(values.shape))
    spots = []
    for shift in (0, 1):
        where = [jax.random.randint(jax.random.fold_in(own_key, axis), (), 0, length) for axis, length in enumerate(values.shape)]
        where[longest] = (where[longest] + shift) % values.shape[longest]
        spots.append(tuple(where))
    return values.at[spots[0]].set(smallest).at[spots[1]].set(high)


def setup_inputs(seed: int = 0) -> dict:
    streams_of = jax.random.split(jax.random.key(seed), 8)
    return {
        "states": set_ends(jax.random.randint(streams_of[0], (NSEQ, L), 0, Q), jax.random.fold_in(streams_of[0], 1), 0, Q - 1).astype(jnp.int32),
        "multiplicity": set_ends(jax.random.randint(streams_of[1], (NSEQ,), 1, 9), jax.random.fold_in(streams_of[1], 1), 1, 8).astype(jnp.int32),
        "fields": draw_fields(jax.random.fold_in(streams_of[7], 71), 0),
        "diag_couplings": draw_diag_couplings(jax.random.fold_in(streams_of[7], 71), 0),
        "slot_couplings": draw_slot_couplings(jax.random.fold_in(streams_of[7], 71), 0),
        "slot_blocks": draw_slot_blocks(jax.random.fold_in(streams_of[7], 71), 0),
        "partner_blocks": draw_partner_blocks(jax.random.fold_in(streams_of[7], 71), 0),
    }


STEP_SIZE = 0.2
THRESHOLD = 0.3

def shrink_groups(values):
    leading = values.shape[:-2]
    grouped = values.reshape(leading + (BLK, Q, BLK, Q))
    square_sums = lax.optimization_barrier(jnp.sum(grouped * grouped, axis=(-3, -1), keepdims=True))
    factor = jnp.maximum(0.0, 1.0 - THRESHOLD / jnp.sqrt(square_sums + 1e-06))
    return (grouped * factor).reshape(values.shape)

def coupling_terms(couplings, column_ids):
    picked = jnp.take(couplings, column_ids, axis=-1)
    return jnp.swapaxes(lax.optimization_barrier(jnp.sum(picked, axis=-1)), -1, -2)

def reference(states, multiplicity, fields, diag_couplings, slot_couplings, slot_blocks, partner_blocks):
    onehot = jax.nn.one_hot(states, Q, dtype=jnp.float32)
    onehot = jnp.transpose(onehot.reshape(NSEQ, NB, K), (1, 0, 2))
    block_states = jnp.transpose(states.reshape(NSEQ, NB, BLK), (1, 0, 2))
    column_ids = (jnp.arange(BLK, dtype=jnp.int32)[None, None, :] * Q + block_states).astype(jnp.int32)
    weight = 1.0 / multiplicity.astype(jnp.float32)
    position = jnp.arange(K) // Q
    off_self = (position[:, None] != position[None, :]).astype(jnp.float32)
    block_ids = jnp.arange(NB, dtype=jnp.int32)
    safe_rows = jnp.maximum(slot_blocks, 0).astype(jnp.int32)
    listed = jnp.any(partner_blocks[safe_rows] == block_ids[:, None, None], axis=-1)
    alive = (slot_blocks >= 0) & listed
    alive_float = alive.astype(jnp.float32)

    def owner_terms(operands):
        couplings, columns = operands
        return coupling_terms(couplings, columns).astype(jnp.bfloat16)
    slot_terms = lax.map(owner_terms, (slot_couplings, column_ids))
    target = jnp.where(alive, slot_blocks, NB).reshape(-1).astype(jnp.int32)
    summed = jax.ops.segment_sum(slot_terms.reshape(NB * SLOTS, NSEQ, K).astype(jnp.float32), target, num_segments=NB + 1)[:NB]

    def self_terms(operands):
        couplings, columns = operands
        return coupling_terms(couplings * off_self, columns)
    own_terms = lax.map(self_terms, (diag_couplings, column_ids))
    logits = fields.reshape(NB, 1, K) + own_terms + summed
    probabilities = jax.nn.softmax(logits.reshape(NB, NSEQ, BLK, Q), axis=-1).reshape(NB, NSEQ, K)
    residual = (weight[None, :, None] * (probabilities - onehot)).astype(jnp.bfloat16)
    residual_wide = residual.astype(jnp.float32)
    grad_fields = lax.optimization_barrier(jnp.sum(residual_wide, axis=1)).reshape(L, Q)
    grad_diag = jnp.einsum('bni,bnk->bik', residual_wide, onehot)

    def owner_grads(operands):
        onehot_owner, row_ids = operands
        picked = residual_wide[row_ids]
        return jnp.einsum('tni,nk->tik', picked, onehot_owner)
    grad_slots = lax.map(owner_grads, (onehot, safe_rows))
    new_diag = off_self * shrink_groups(diag_couplings - STEP_SIZE * grad_diag)
    new_slots = alive_float[:, :, None, None] * shrink_groups(slot_couplings - STEP_SIZE * grad_slots)
    new_fields = fields - STEP_SIZE * grad_fields
    return (new_fields, new_diag, new_slots)
```

```python
import functools
import jax
import jax.numpy as jnp
from jax import lax
from jax.experimental import pallas as pl
from jax.experimental.pallas import tpu as pltpu
from jax.sharding import PartitionSpec as P

STEP_SIZE = 0.2
THRESHOLD = 0.3
HIGHEST_MODE = lax.Precision.HIGHEST
F32 = jnp.float32
BF16 = jnp.bfloat16


def halves(values):
    high = values.astype(BF16)
    return high, (values - high.astype(F32)).astype(BF16)


def times(left, right):
    return jnp.dot(left, right, preferred_element_type=F32)


def indicator(rows, columns, states_count):
    row = lax.broadcasted_iota(jnp.int32, (rows, columns), 0)
    column = lax.broadcasted_iota(jnp.int32, (rows, columns), 1)
    return jnp.where((column >= row * states_count) & (column < (row + 1) * states_count), 1.0, 0.0).astype(BF16)


def indicator_t(rows, columns, states_count):
    row = lax.broadcasted_iota(jnp.int32, (rows, columns), 0)
    column = lax.broadcasted_iota(jnp.int32, (rows, columns), 1)
    return jnp.where((row >= column * states_count) & (row < (column + 1) * states_count), 1.0, 0.0).astype(BF16)


def step_kernel(
    block_len, states_count, slots,
    ids_ref, alive_ref, resid_ref, states_ref, fields_ref, diag_ref, slot_ref,
    new_fields_ref, new_diag_ref, new_slots_ref, onehot_ref,
):
    width = block_len * states_count
    step = pl.program_id(0)
    groups = indicator(block_len, width, states_count)
    groups_t = indicator_t(width, block_len, states_count)

    @pl.when(step == 0)
    def _():
        spread = times(states_ref[...].astype(F32).astype(BF16), groups)
        column = lax.broadcasted_iota(jnp.int32, (1, width), 1)
        start = jnp.zeros((1, width), jnp.int32)
        for p in range(1, block_len):
            start = jnp.where(column >= p * states_count, p * states_count, start)
        onehot_ref[...] = jnp.where(spread == (column - start).astype(F32), 1.0, 0.0).astype(BF16)

    resid = resid_ref[...].reshape(-1, width)
    grad = lax.dot_general(
        resid, onehot_ref[...], (((0,), (0,)), ((), ())), preferred_element_type=F32
    )

    def factors(values):
        high, low = halves(values * values)
        sums = times(groups, high) + times(groups, low)
        high, low = halves(sums)
        sums = times(high, groups_t) + times(low, groups_t)
        factor = jnp.maximum(0.0, 1.0 - THRESHOLD / jnp.sqrt(sums + 1e-06))
        return factor

    def expand(factor):
        high, low = halves(factor)
        wide = times(high, groups) + times(low, groups)
        high, low = halves(wide)
        return times(groups_t, high) + times(groups_t, low)

    @pl.when(step < slots)
    def _():
        values = slot_ref[0, 0] - STEP_SIZE * grad
        keep = alive_ref[step].astype(F32)
        new_slots_ref[0, 0] = values * expand(factors(values) * keep)

    @pl.when(step == slots)
    def _():
        values = diag_ref[0] - STEP_SIZE * grad
        row = lax.broadcasted_iota(jnp.int32, (block_len, block_len), 0)
        column = lax.broadcasted_iota(jnp.int32, (block_len, block_len), 1)
        factor = jnp.where(row == column, 0.0, factors(values))
        new_diag_ref[0] = values * expand(factor)
        ones = jnp.ones((8, resid.shape[0]), BF16)
        new_fields_ref[...] = fields_ref[...] - STEP_SIZE * times(ones, resid)[:1]


def apply_step(ids, alive, gathered, states_all, fields, diag_couplings, slot_couplings):
    seqs, blocks, seq_rows, width = gathered.shape
    slots = slot_couplings.shape[1]
    block_len, states_count = fields.shape
    last = slots - 1
    spec = pltpu.PrefetchScalarGridSpec(
        num_scalar_prefetch=2,
        grid=(slots + 1,),
        in_specs=[
            pl.BlockSpec((seqs, 1, seq_rows, width), lambda i, ids, alive: (0, ids[i], 0, 0)),
            pl.BlockSpec(states_all.shape, lambda i, ids, alive: (0, 0)),
            pl.BlockSpec((1, width), lambda i, ids, alive: (0, 0)),
            pl.BlockSpec((1, width, width), lambda i, ids, alive: (0, 0, 0)),
            pl.BlockSpec((1, 1, width, width), lambda i, ids, alive: (0, jnp.minimum(i, last), 0, 0)),
        ],
        out_specs=[
            pl.BlockSpec((1, width), lambda i, ids, alive: (0, 0)),
            pl.BlockSpec((1, width, width), lambda i, ids, alive: (0, 0, 0)),
            pl.BlockSpec((1, 1, width, width), lambda i, ids, alive: (0, jnp.minimum(i, last), 0, 0)),
        ],
        scratch_shapes=[pltpu.VMEM((states_all.shape[0], width), BF16)],
    )
    new_fields, new_diag, new_slots = pl.pallas_call(
        functools.partial(step_kernel, block_len, states_count, slots),
        grid_spec=spec,
        out_shape=[
            jax.ShapeDtypeStruct((1, width), F32),
            jax.ShapeDtypeStruct(diag_couplings.shape, F32),
            jax.ShapeDtypeStruct(slot_couplings.shape, F32),
        ],
        compiler_params=pltpu.CompilerParams(vmem_limit_bytes=40 * 1024 * 1024),
    )(ids, alive, gathered, states_all, fields.reshape(1, width), diag_couplings, slot_couplings)
    return new_fields.reshape(block_len, states_count), new_diag, new_slots


def per_device(
    states, multiplicity, fields, diag_couplings, slot_couplings, slot_blocks, partner_blocks
):
    seq_rows, block_len = states.shape
    states_count = fields.shape[1]
    row_width = block_len * states_count
    blocks = lax.axis_size("pos")
    my_block = lax.axis_index("pos")
    states_all = lax.all_gather(states, "seq", axis=0, tiled=True)
    onehot_wide = jax.nn.one_hot(states, states_count, dtype=F32).reshape(seq_rows, row_width)
    weight = 1.0 / multiplicity.astype(F32)
    position = jnp.arange(row_width) // states_count
    off_self = (position[:, None] != position[None, :]).astype(F32)
    my_slots = lax.dynamic_index_in_dim(slot_blocks, my_block, axis=0, keepdims=False)
    row_ids = jnp.maximum(my_slots, 0)
    partners = jnp.take(partner_blocks, row_ids, axis=0)
    alive = (my_slots >= 0) & jnp.any(partners == my_block, axis=1)
    block_ids = jnp.arange(blocks, dtype=jnp.int32)
    slot_pick = ((my_slots[:, None] == block_ids[None, :]) & alive[:, None]).astype(BF16)
    slot_terms = jnp.einsum(
        "nk,tik->tni", onehot_wide, slot_couplings[0], precision=HIGHEST_MODE
    ).astype(BF16)
    outgoing = jnp.einsum("td,tnk->dnk", slot_pick, slot_terms, preferred_element_type=BF16)
    arrived = lax.all_to_all(outgoing, "pos", split_axis=0, concat_axis=0, tiled=True)
    source_ones = jnp.ones((arrived.shape[0],), BF16)
    incoming = jnp.einsum("d,dnk->nk", source_ones, arrived, preferred_element_type=F32)
    own_terms = jnp.einsum(
        "nk,ik->ni", onehot_wide, diag_couplings[0] * off_self, precision=HIGHEST_MODE
    )
    logits = fields.reshape(1, row_width) + own_terms + incoming
    probabilities = jax.nn.softmax(
        logits.reshape(seq_rows, block_len, states_count), axis=-1
    ).reshape(seq_rows, row_width)
    residual = (weight[:, None] * (probabilities - onehot_wide)).astype(BF16)
    block_resid = lax.all_gather(residual, "pos", axis=0, tiled=False)
    ids = jnp.concatenate([row_ids, my_block[None].astype(jnp.int32)])
    wanted = jnp.concatenate(
        [lax.dynamic_index_in_dim(block_resid, ids[t], axis=0) for t in range(ids.shape[0])]
    )
    gathered = lax.all_gather(wanted, "seq", axis=0, tiled=False)
    ids = jnp.arange(ids.shape[0], dtype=jnp.int32)
    return apply_step(
        ids, alive.astype(jnp.int32), gathered, states_all, fields, diag_couplings, slot_couplings
    )


def solution(mesh):
    placed = (
        P("seq", "pos"),
        P("seq"),
        P("pos", None),
        P("pos", None, None),
        P("pos", None, None, None),
        P(),
        P(),
    )
    return jax.shard_map(
        per_device,
        mesh=mesh,
        in_specs=placed,
        out_specs=(P("pos", None), P("pos", None, None), P("pos", None, None, None)),
        check_vma=False,
    )
```

```python
import functools
import jax
import jax.numpy as jnp
from jax import lax
from jax.experimental import pallas as pl
from jax.experimental.pallas import tpu as pltpu
from jax.sharding import PartitionSpec as P

STEP_SIZE = 0.2
THRESHOLD = 0.3
F32 = jnp.float32
BF16 = jnp.bfloat16


def halves(values):
    high = values.astype(BF16)
    return high, (values - high.astype(F32)).astype(BF16)


def times(left, right):
    return jnp.dot(left, right, preferred_element_type=F32)


def indicator(rows, columns, states_count):
    row = lax.broadcasted_iota(jnp.int32, (rows, columns), 0)
    column = lax.broadcasted_iota(jnp.int32, (rows, columns), 1)
    return jnp.where((column >= row * states_count) & (column < (row + 1) * states_count), 1.0, 0.0).astype(BF16)


def indicator_t(rows, columns, states_count):
    row = lax.broadcasted_iota(jnp.int32, (rows, columns), 0)
    column = lax.broadcasted_iota(jnp.int32, (rows, columns), 1)
    return jnp.where((row >= column * states_count) & (row < (column + 1) * states_count), 1.0, 0.0).astype(BF16)


def position_starts(block_len, states_count):
    column = lax.broadcasted_iota(jnp.int32, (1, block_len * states_count), 1)
    start = jnp.zeros_like(column)
    for p in range(1, block_len):
        start = jnp.where(column >= p * states_count, p * states_count, start)
    return column, start


def onehot_of(states_t, groups, column, start):
    spread = lax.dot_general(
        states_t, groups, (((0,), (0,)), ((), ())), preferred_element_type=F32
    )
    return jnp.where(spread == (column - start).astype(F32), 1.0, 0.0).astype(BF16)


def exchange_kernel(
    block_len, states_count, seqs, highs, lows,
    slot_blocks_ref, partner_ref, states_ref, multiplicity_ref, fields_ref, diag_ref, slot_ref,
    out_ref, states_out_ref,
    term_ref, near_ref, high1_ref, stage1_ref, low1_ref, high2_ref, stage2_ref, low2_ref,
    send_sem, recv_sem,
):
    width = block_len * states_count
    slots = slot_ref.shape[1]
    far = slots - 2
    blocks = highs * lows
    seq = lax.axis_index("seq")
    pos = lax.axis_index("pos")
    high = pos // lows
    low = pos % lows

    def place(f, target):
        return (lax.rem(seq + f, seqs), target)

    def beside(g):
        return lax.rem(pos + g + blocks, blocks)

    def high_peer(d):
        return lax.rem(high + d, highs) * lows + low

    def low_peer(e):
        return high * lows + lax.rem(low + e, lows)

    near = [(f, g) for g in (0, 1, -1) for f in range(seqs) if (f, g) != (0, 0)]
    peers = [place(f, beside(g)) for f, g in near]
    peers += [place(0, high_peer(d)) for d in range(1, highs)]
    peers += [place(0, low_peer(e)) for e in range(1, lows)]
    barrier = pltpu.get_barrier_semaphore()
    for peer in peers:
        pl.semaphore_signal(barrier, inc=1, device_id=peer, device_id_type=pl.DeviceIdType.MESH)

    groups = indicator(block_len, width, states_count)
    column, start = position_starts(block_len, states_count)
    onehot = onehot_of(states_ref[...], groups, column, start)

    def terms(values):
        first = values.astype(BF16)
        rest = values - first.astype(F32)
        second = rest.astype(BF16)
        third = (rest - second.astype(F32)).astype(BF16)
        total = None
        for part in (third, second, first):
            product = lax.dot_general(
                onehot, part, (((1,), (1,)), ((), ())), preferred_element_type=F32
            )
            total = product if total is None else total + product
        return total

    copies = []

    def send(source, target, device):
        k = len(copies)
        copy = pltpu.make_async_remote_copy(
            src_ref=source, dst_ref=target, send_sem=send_sem.at[k], recv_sem=recv_sem.at[k],
            device_id=device, device_id_type=pl.DeviceIdType.MESH,
        )
        copy.start()
        copies.append(copy)
        return copy

    for t in range(far):
        high1_ref[0, t] = terms(slot_ref[0, 2 + t]).astype(BF16)
    states_out_ref[0] = states_ref[...]
    pl.semaphore_wait(barrier, len(peers))
    high1 = [
        send(high1_ref.at[0], high1_ref.at[d], place(0, high_peer(d))) for d in range(1, highs)
    ]
    for t in range(2):
        term_ref[t] = terms(slot_ref[0, t]).astype(BF16)
    near1 = [
        send(term_ref.at[0], near_ref.at[0], place(0, beside(-1))),
        send(term_ref.at[1], near_ref.at[1], place(0, beside(1))),
    ]
    states_moves = [
        send(states_ref, states_out_ref.at[f], place(f, pos)) for f in range(1, seqs)
    ]
    mask = jnp.zeros((width, width), jnp.bool_)
    row = lax.broadcasted_iota(jnp.int32, (width, width), 0)
    wide = lax.broadcasted_iota(jnp.int32, (width, width), 1)
    for p in range(block_len):
        lo, hi = p * states_count, (p + 1) * states_count
        mask = mask | ((row >= lo) & (row < hi) & (wide >= lo) & (wide < hi))
    logits = fields_ref[...] + terms(jnp.where(mask, 0.0, diag_ref[0]))
    same = jnp.where(mask, 1.0, 0.0).astype(BF16)

    def search(target, t):
        def one(c, found):
            return jnp.where(slot_blocks_ref[c, t] == target, c, found)

        return lax.fori_loop(0, blocks, one, jnp.int32(-1))

    def listed(holder):
        hit = partner_ref[pos, 0] == holder
        for k in range(1, slots):
            hit = hit | (partner_ref[pos, k] == holder)
        return jnp.where(hit & (holder >= 0), 1.0, 0.0).astype(F32)

    holders = [search(pos, t) for t in range(slots)]

    def ring(value, size):
        return lax.rem(value + size, size)

    for copy in high1:
        copy.wait_recv()
    low1 = []
    for e in list(range(1, lows)) + [0]:
        for t in range(far):
            target = low_peer(e)
            pick = jnp.int32(0)
            for h in range(highs):
                found = slot_blocks_ref[h * lows + low, 2 + t] == target
                pick = jnp.where(found, ring(high - h, highs), pick)
            value = high1_ref[pick, t]
            if e == 0:
                low1_ref[0, t] = value
            else:
                stage1_ref[e, t] = value
        if e:
            low1.append(send(stage1_ref.at[e], low1_ref.at[e], place(0, target)))
    for copy in near1:
        copy.wait_recv()
    incoming = near_ref[0].astype(F32) * listed(holders[0])
    incoming += near_ref[1].astype(F32) * listed(holders[1])
    for copy in low1:
        copy.wait_recv()
    for t in range(far):
        holder = holders[2 + t]
        pick = ring(low - lax.rem(jnp.maximum(holder, 0), lows), lows)
        incoming += low1_ref[pick, t].astype(F32) * listed(holder)
    logits += incoming

    peak = jnp.zeros_like(logits)
    for p in range(block_len):
        inside = start == p * states_count
        top = jnp.max(jnp.where(inside, logits, -jnp.inf), axis=1, keepdims=True)
        peak = jnp.where(inside, top, peak)
    powers = jnp.exp(logits - peak)
    first, second = halves(powers)
    probabilities = powers / (times(first, same) + times(second, same))
    weight = 1.0 / multiplicity_ref[...]
    residual = (weight * (probabilities - onehot.astype(F32))).astype(BF16)
    high2_ref[0] = residual
    out_ref[0, slots] = residual

    high2 = [
        send(high2_ref.at[0], high2_ref.at[d], place(0, high_peer(d))) for d in range(1, highs)
    ]
    slot_of = {0: slots, 1: 0, -1: 1}
    last = [
        send(high2_ref.at[0], out_ref.at[f, slot_of[g]], place(f, beside(g))) for f, g in near
    ]
    for copy in high2:
        copy.wait_recv()
    low2 = []
    for e in list(range(1, lows)) + [0]:
        for t in range(far):
            target = low_peer(e)
            wanted = jnp.maximum(slot_blocks_ref[target, 2 + t], 0)
            value = high2_ref[ring(high - wanted // lows, highs)]
            if e == 0:
                low2_ref[0, t] = value
            else:
                stage2_ref[e, t] = value
        if e:
            low2.append(send(stage2_ref.at[e], low2_ref.at[e], place(0, target)))
    for copy in low2:
        copy.wait_recv()
    for t in range(far):
        wanted = jnp.maximum(slot_blocks_ref[pos, 2 + t], 0)
        out_ref[0, 2 + t] = low2_ref[ring(low - lax.rem(wanted, lows), lows), t]
    last += [
        send(out_ref.at[0, pl.ds(2, far)], out_ref.at[f, pl.ds(2, far)], place(f, pos))
        for f in range(1, seqs)
    ]
    for copy in states_moves + last:
        copy.wait_recv()
    for copy in copies:
        copy.wait_send()


def exchange(slot_blocks, partner_blocks, states_t, multiplicity, fields, diag, slot):
    block_len, seq_rows = states_t.shape
    width = fields.shape[1]
    slots = slot.shape[1]
    seqs, blocks = lax.axis_size("seq"), lax.axis_size("pos")
    lows = 4 if blocks % 4 == 0 else 1
    highs = blocks // lows
    moves = 2 * (highs - 1) + 2 * (lows - 1) + 2 + (seqs - 1) * 2 + 3 * seqs
    vmem = pl.BlockSpec(memory_space=pltpu.VMEM)
    smem = pl.BlockSpec(memory_space=pltpu.SMEM)
    far = slots - 2
    tile = (seq_rows, width)
    return pl.pallas_call(
        functools.partial(exchange_kernel, block_len, width // block_len, seqs, highs, lows),
        in_specs=[smem, smem, vmem, vmem, vmem, vmem, vmem],
        out_specs=[vmem, vmem],
        out_shape=[
            jax.ShapeDtypeStruct((seqs, slots + 1) + tile, BF16),
            jax.ShapeDtypeStruct((seqs, block_len, seq_rows), BF16),
        ],
        scratch_shapes=[
            pltpu.VMEM((2,) + tile, BF16),
            pltpu.VMEM((2,) + tile, BF16),
            pltpu.VMEM((highs, far) + tile, BF16),
            pltpu.VMEM((lows, far) + tile, BF16),
            pltpu.VMEM((lows, far) + tile, BF16),
            pltpu.VMEM((highs,) + tile, BF16),
            pltpu.VMEM((lows, far) + tile, BF16),
            pltpu.VMEM((lows, far) + tile, BF16),
            pltpu.SemaphoreType.DMA((moves,)),
            pltpu.SemaphoreType.DMA((moves,)),
        ],
        compiler_params=pltpu.CompilerParams(
            collective_id=0, has_side_effects=True, vmem_limit_bytes=48 * 1024 * 1024
        ),
    )(slot_blocks, partner_blocks, states_t, multiplicity, fields, diag, slot)


def step_kernel(
    block_len, states_count, slots,
    slot_blocks_ref, partner_ref, resid_ref, states_ref, fields_ref, diag_ref, slot_ref,
    new_fields_ref, new_diag_ref, new_slots_ref, onehot_ref,
):
    width = block_len * states_count
    step = pl.program_id(0)
    groups = indicator(block_len, width, states_count)
    groups_t = indicator_t(width, block_len, states_count)

    @pl.when(step == 0)
    def _():
        column, start = position_starts(block_len, states_count)
        seq_rows = states_ref.shape[2]
        for f in range(states_ref.shape[0]):
            onehot_ref[pl.ds(f * seq_rows, seq_rows)] = onehot_of(
                states_ref[f], groups, column, start
            )

    resid = resid_ref[...].reshape(-1, width)
    grad = lax.dot_general(
        resid, onehot_ref[...], (((0,), (0,)), ((), ())), preferred_element_type=F32
    )

    def factors(values):
        high, low = halves(values * values)
        sums = times(groups, high) + times(groups, low)
        high, low = halves(sums)
        sums = times(high, groups_t) + times(low, groups_t)
        factor = jnp.maximum(0.0, 1.0 - THRESHOLD / jnp.sqrt(sums + 1e-06))
        return factor

    def expand(factor):
        high, low = halves(factor)
        wide = times(high, groups) + times(low, groups)
        high, low = halves(wide)
        return times(groups_t, high) + times(groups_t, low)

    @pl.when(step < slots)
    def _():
        values = slot_ref[0, 0] - STEP_SIZE * grad
        me = lax.axis_index("pos")
        holder = slot_blocks_ref[me, step]
        listing = jnp.maximum(holder, 0)
        hit = partner_ref[listing, 0] == me
        for k in range(1, slots):
            hit = hit | (partner_ref[listing, k] == me)
        keep = jnp.where(hit & (holder >= 0), 1.0, 0.0).astype(F32)
        new_slots_ref[0, 0] = values * expand(factors(values) * keep)

    @pl.when(step == slots)
    def _():
        values = diag_ref[0] - STEP_SIZE * grad
        row = lax.broadcasted_iota(jnp.int32, (block_len, block_len), 0)
        column = lax.broadcasted_iota(jnp.int32, (block_len, block_len), 1)
        factor = jnp.where(row == column, 0.0, factors(values))
        new_diag_ref[0] = values * expand(factor)
        ones = jnp.ones((8, resid.shape[0]), BF16)
        new_fields_ref[...] = fields_ref[...] - STEP_SIZE * times(ones, resid)[:1]


def apply_step(slot_blocks, partner_blocks, gathered, states_all, fields, diag_couplings, slot_couplings):
    seqs, _, seq_rows, width = gathered.shape
    slots = slot_couplings.shape[1]
    block_len = states_all.shape[1]
    states_count = width // block_len
    last = slots - 1
    spec = pltpu.PrefetchScalarGridSpec(
        num_scalar_prefetch=2,
        grid=(slots + 1,),
        in_specs=[
            pl.BlockSpec((seqs, 1, seq_rows, width), lambda i, ids, alive: (0, i, 0, 0)),
            pl.BlockSpec(states_all.shape, lambda i, ids, alive: (0, 0, 0)),
            pl.BlockSpec((1, width), lambda i, ids, alive: (0, 0)),
            pl.BlockSpec((1, width, width), lambda i, ids, alive: (0, 0, 0)),
            pl.BlockSpec((1, 1, width, width), lambda i, ids, alive: (0, jnp.minimum(i, last), 0, 0)),
        ],
        out_specs=[
            pl.BlockSpec((1, width), lambda i, ids, alive: (0, 0)),
            pl.BlockSpec((1, width, width), lambda i, ids, alive: (0, 0, 0)),
            pl.BlockSpec((1, 1, width, width), lambda i, ids, alive: (0, jnp.minimum(i, last), 0, 0)),
        ],
        scratch_shapes=[pltpu.VMEM((seqs * seq_rows, width), BF16)],
    )
    new_fields, new_diag, new_slots = pl.pallas_call(
        functools.partial(step_kernel, block_len, states_count, slots),
        grid_spec=spec,
        out_shape=[
            jax.ShapeDtypeStruct((1, width), F32),
            jax.ShapeDtypeStruct(diag_couplings.shape, F32),
            jax.ShapeDtypeStruct(slot_couplings.shape, F32),
        ],
        compiler_params=pltpu.CompilerParams(vmem_limit_bytes=40 * 1024 * 1024),
    )(slot_blocks, partner_blocks, gathered, states_all, fields, diag_couplings, slot_couplings)
    return new_fields.reshape(block_len, states_count), new_diag, new_slots


def per_device(
    states, multiplicity, fields, diag_couplings, slot_couplings, slot_blocks, partner_blocks
):
    fields_row = fields.reshape(1, -1)
    gathered, states_all = exchange(
        slot_blocks,
        partner_blocks,
        states.T.astype(BF16),
        multiplicity.astype(F32)[:, None],
        fields_row,
        diag_couplings,
        slot_couplings,
    )
    return apply_step(
        slot_blocks, partner_blocks, gathered, states_all, fields_row, diag_couplings, slot_couplings
    )


def solution(mesh):
    placed = (
        P("seq", "pos"),
        P("seq"),
        P("pos", None),
        P("pos", None, None),
        P("pos", None, None, None),
        P(),
        P(),
    )
    return jax.shard_map(
        per_device,
        mesh=mesh,
        in_specs=placed,
        out_specs=(P("pos", None), P("pos", None, None), P("pos", None, None, None)),
        check_vma=False,
    )
```

```python
import functools
import jax
import jax.numpy as jnp
from jax import lax
from jax.experimental import pallas as pl
from jax.experimental.pallas import tpu as pltpu
from jax.sharding import PartitionSpec as P

STEP_SIZE = 0.2
THRESHOLD = 0.3
F32 = jnp.float32
BF16 = jnp.bfloat16


def halves(values):
    high = values.astype(BF16)
    return high, (values - high.astype(F32)).astype(BF16)


def times(left, right):
    return jnp.dot(left, right, preferred_element_type=F32)


def indicator(rows, columns, states_count):
    row = lax.broadcasted_iota(jnp.int32, (rows, columns), 0)
    column = lax.broadcasted_iota(jnp.int32, (rows, columns), 1)
    return jnp.where((column >= row * states_count) & (column < (row + 1) * states_count), 1.0, 0.0).astype(BF16)


def indicator_t(rows, columns, states_count):
    row = lax.broadcasted_iota(jnp.int32, (rows, columns), 0)
    column = lax.broadcasted_iota(jnp.int32, (rows, columns), 1)
    return jnp.where((row >= column * states_count) & (row < (column + 1) * states_count), 1.0, 0.0).astype(BF16)


def position_starts(block_len, states_count):
    column = lax.broadcasted_iota(jnp.int32, (1, block_len * states_count), 1)
    start = jnp.zeros_like(column)
    for p in range(1, block_len):
        start = jnp.where(column >= p * states_count, p * states_count, start)
    return column, start


def onehot_of(states_t, groups, column, start):
    spread = lax.dot_general(
        states_t, groups, (((0,), (0,)), ((), ())), preferred_element_type=F32
    )
    return jnp.where(spread == (column - start).astype(F32), 1.0, 0.0).astype(BF16)


def exchange_kernel(
    block_len, states_count, seqs, highs, lows,
    slot_blocks_ref, partner_ref, states_ref, multiplicity_ref, fields_ref, diag_ref, slot_ref,
    out_ref, states_out_ref,
    term_ref, near_ref, high1_ref, stage1_ref, low1_ref, high2_ref, stage2_ref, low2_ref,
    logits_ref, send_sem, recv_sem,
):
    width = block_len * states_count
    slots = slot_ref.shape[1]
    far = slots - 2
    blocks = highs * lows
    seq = lax.axis_index("seq")
    pos = lax.axis_index("pos")
    high = pos // lows
    low = pos % lows

    def place(f, target):
        return (lax.rem(seq + f, seqs), target)

    def beside(g):
        return lax.rem(pos + g + blocks, blocks)

    def high_peer(d):
        return lax.rem(high + d, highs) * lows + low

    def low_peer(e):
        return high * lows + lax.rem(low + e, lows)

    near = [(f, g) for g in (0, 1, -1) for f in range(seqs) if (f, g) != (0, 0)]
    peers = [place(f, beside(g)) for f, g in near]
    peers += [place(0, high_peer(d)) for d in range(1, highs)]
    peers += [place(0, low_peer(e)) for e in range(1, lows)]
    barrier = pltpu.get_barrier_semaphore()
    for peer in peers:
        pl.semaphore_signal(barrier, inc=1, device_id=peer, device_id_type=pl.DeviceIdType.MESH)

    groups = indicator(block_len, width, states_count)
    column, start = position_starts(block_len, states_count)
    onehot = onehot_of(states_ref[...], groups, column, start)

    def terms(values):
        first = values.astype(BF16)
        rest = values - first.astype(F32)
        second = rest.astype(BF16)
        third = (rest - second.astype(F32)).astype(BF16)
        total = None
        for part in (third, second, first):
            product = lax.dot_general(
                onehot, part, (((1,), (1,)), ((), ())), preferred_element_type=F32
            )
            total = product if total is None else total + product
        return total

    copies = []

    def send(source, target, device):
        k = len(copies)
        copy = pltpu.make_async_remote_copy(
            src_ref=source, dst_ref=target, send_sem=send_sem.at[k], recv_sem=recv_sem.at[k],
            device_id=device, device_id_type=pl.DeviceIdType.MESH,
        )
        copy.start()
        copies.append(copy)
        return copy

    rows = states_ref.shape[1]
    chunks = len(high1_ref)
    depth = rows // chunks
    parts = [pl.ds(r * depth, depth) for r in range(chunks)]

    for t in range(far):
        value = terms(slot_ref[0, 2 + t]).astype(BF16)
        for r in range(chunks):
            high1_ref[r][0, t] = value[r * depth : (r + 1) * depth]
    states_out_ref[0] = states_ref[...]
    pl.semaphore_wait(barrier, len(peers))
    high1 = [
        [
            send(high1_ref[r].at[0], high1_ref[r].at[d], place(0, high_peer(d)))
            for d in range(1, highs)
        ]
        for r in range(chunks)
    ]
    for t in range(2):
        term_ref[t] = terms(slot_ref[0, t]).astype(BF16)
    near1 = [
        send(term_ref.at[0], near_ref.at[0], place(0, beside(-1))),
        send(term_ref.at[1], near_ref.at[1], place(0, beside(1))),
    ]
    states_moves = [
        send(states_ref, states_out_ref.at[f], place(f, pos)) for f in range(1, seqs)
    ]
    mask = jnp.zeros((width, width), jnp.bool_)
    row = lax.broadcasted_iota(jnp.int32, (width, width), 0)
    wide = lax.broadcasted_iota(jnp.int32, (width, width), 1)
    for p in range(block_len):
        lo, hi = p * states_count, (p + 1) * states_count
        mask = mask | ((row >= lo) & (row < hi) & (wide >= lo) & (wide < hi))
    logits_ref[...] = fields_ref[...] + terms(jnp.where(mask, 0.0, diag_ref[0]))
    same = jnp.where(mask, 1.0, 0.0).astype(BF16)

    def search(target, t):
        def one(c, found):
            return jnp.where(slot_blocks_ref[c, t] == target, c, found)

        return lax.fori_loop(0, blocks, one, jnp.int32(-1))

    def listed(holder):
        hit = partner_ref[pos, 0] == holder
        for k in range(1, slots):
            hit = hit | (partner_ref[pos, k] == holder)
        return jnp.where(hit & (holder >= 0), 1.0, 0.0).astype(F32)

    def ring(value, size):
        return lax.rem(value + size, size)

    holders = [search(pos, t) for t in range(slots)]
    alive = [listed(holder) for holder in holders]
    order = list(range(1, lows)) + [0]
    picks1, picks2 = {}, {}
    for e in order:
        target = low_peer(e)
        for t in range(far):
            pick = jnp.int32(0)
            for h in range(highs):
                found = slot_blocks_ref[h * lows + low, 2 + t] == target
                pick = jnp.where(found, ring(high - h, highs), pick)
            picks1[e, t] = pick
            wanted = jnp.maximum(slot_blocks_ref[target, 2 + t], 0)
            picks2[e, t] = ring(high - wanted // lows, highs)
    weight = 1.0 / multiplicity_ref[...]

    def pass_low(load, stage_ref, low_ref):
        sent = []
        for e in order:
            for t in range(far):
                value = load(e, t)
                if e == 0:
                    low_ref[0, t] = value
                else:
                    stage_ref[e, t] = value
            if e:
                sent.append(
                    send(
                        stage_ref.at[e],
                        low_ref.at[e],
                        place(0, low_peer(e)),
                    )
                )
        return sent

    low1 = []
    for r in range(chunks):
        for copy in high1[r]:
            copy.wait_recv()
        low1.append(
            pass_low(lambda e, t: high1_ref[r][picks1[e, t], t], stage1_ref[r], low1_ref[r])
        )
    for copy in near1:
        copy.wait_recv()
    slot_of = {0: slots, 1: 0, -1: 1}
    high2, last = [], []
    column_start = start
    for r, part in enumerate(parts):
        logits = logits_ref[part] + near_ref[0, part].astype(F32) * alive[0]
        logits += near_ref[1, part].astype(F32) * alive[1]
        for copy in low1[r]:
            copy.wait_recv()
        for t in range(far):
            holder = jnp.maximum(holders[2 + t], 0)
            pick = ring(low - lax.rem(holder, lows), lows)
            logits += low1_ref[r][pick, t].astype(F32) * alive[2 + t]
        peak = jnp.zeros_like(logits)
        for p in range(block_len):
            inside = column_start == p * states_count
            top = jnp.max(jnp.where(inside, logits, -jnp.inf), axis=1, keepdims=True)
            peak = jnp.where(inside, top, peak)
        powers = jnp.exp(logits - peak)
        first, second = halves(powers)
        probabilities = powers / (times(first, same) + times(second, same))
        mine = slice(r * depth, (r + 1) * depth)
        residual = (weight[mine] * (probabilities - onehot[mine].astype(F32))).astype(BF16)
        high2_ref[r][0] = residual
        out_ref[0, slots, part] = residual
        high2.append(
            [
                send(high2_ref[r].at[0], high2_ref[r].at[d], place(0, high_peer(d)))
                for d in range(1, highs)
            ]
        )
        last += [
            send(high2_ref[r].at[0], out_ref.at[f, slot_of[g], part], place(f, beside(g)))
            for f, g in near
        ]
    low2 = []
    for r in range(chunks):
        for copy in high2[r]:
            copy.wait_recv()
        low2.append(
            pass_low(lambda e, t: high2_ref[r][picks2[e, t]], stage2_ref[r], low2_ref[r])
        )
    ends = pl.ds(2, far)
    for r, part in enumerate(parts):
        for copy in low2[r]:
            copy.wait_recv()
        for t in range(far):
            wanted = jnp.maximum(slot_blocks_ref[pos, 2 + t], 0)
            pick = ring(low - lax.rem(wanted, lows), lows)
            out_ref[0, 2 + t, part] = low2_ref[r][pick, t]
        last += [
            send(out_ref.at[0, ends, part], out_ref.at[f, ends, part], place(f, pos))
            for f in range(1, seqs)
        ]
    for copy in states_moves + last:
        copy.wait_recv()
    for copy in copies:
        copy.wait_send()


def exchange(slot_blocks, partner_blocks, states_t, multiplicity, fields, diag, slot):
    block_len, seq_rows = states_t.shape
    width = fields.shape[1]
    slots = slot.shape[1]
    seqs, blocks = lax.axis_size("seq"), lax.axis_size("pos")
    lows = 4 if blocks % 4 == 0 else 1
    highs = blocks // lows
    moves = 4 * (highs - 1) + 4 * (lows - 1) + 9 * seqs
    vmem = pl.BlockSpec(memory_space=pltpu.VMEM)
    smem = pl.BlockSpec(memory_space=pltpu.SMEM)
    far = slots - 2
    tile = (seq_rows, width)
    chunks = 2 if seq_rows % 32 == 0 else 1
    piece = (seq_rows // chunks, width)
    return pl.pallas_call(
        functools.partial(exchange_kernel, block_len, width // block_len, seqs, highs, lows),
        in_specs=[smem, smem, vmem, vmem, vmem, vmem, vmem],
        out_specs=[vmem, vmem],
        out_shape=[
            jax.ShapeDtypeStruct((seqs, slots + 1) + tile, BF16),
            jax.ShapeDtypeStruct((seqs, block_len, seq_rows), BF16),
        ],
        scratch_shapes=[
            pltpu.VMEM((2,) + tile, BF16),
            pltpu.VMEM((2,) + tile, BF16),
            [pltpu.VMEM((highs, far) + piece, BF16)] * chunks,
            [pltpu.VMEM((lows, far) + piece, BF16)] * chunks,
            [pltpu.VMEM((lows, far) + piece, BF16)] * chunks,
            [pltpu.VMEM((highs,) + piece, BF16)] * chunks,
            [pltpu.VMEM((lows, far) + piece, BF16)] * chunks,
            [pltpu.VMEM((lows, far) + piece, BF16)] * chunks,
            pltpu.VMEM(tile, F32),
            pltpu.SemaphoreType.DMA((moves,)),
            pltpu.SemaphoreType.DMA((moves,)),
        ],
        compiler_params=pltpu.CompilerParams(
            collective_id=0, has_side_effects=True, vmem_limit_bytes=48 * 1024 * 1024
        ),
    )(slot_blocks, partner_blocks, states_t, multiplicity, fields, diag, slot)


def step_kernel(
    block_len, states_count, slots,
    slot_blocks_ref, partner_ref, resid_ref, states_ref, fields_ref, diag_ref, slot_ref,
    new_fields_ref, new_diag_ref, new_slots_ref, onehot_ref,
):
    width = block_len * states_count
    step = pl.program_id(0)
    groups = indicator(block_len, width, states_count)
    groups_t = indicator_t(width, block_len, states_count)

    @pl.when(step == 0)
    def _():
        column, start = position_starts(block_len, states_count)
        seq_rows = states_ref.shape[2]
        for f in range(states_ref.shape[0]):
            onehot_ref[pl.ds(f * seq_rows, seq_rows)] = onehot_of(
                states_ref[f], groups, column, start
            )

    resid = resid_ref[...].reshape(-1, width)
    grad = lax.dot_general(
        resid, onehot_ref[...], (((0,), (0,)), ((), ())), preferred_element_type=F32
    )

    def factors(values):
        high, low = halves(values * values)
        sums = times(groups, high) + times(groups, low)
        high, low = halves(sums)
        sums = times(high, groups_t) + times(low, groups_t)
        factor = jnp.maximum(0.0, 1.0 - THRESHOLD / jnp.sqrt(sums + 1e-06))
        return factor

    def expand(factor):
        high, low = halves(factor)
        wide = times(high, groups) + times(low, groups)
        high, low = halves(wide)
        return times(groups_t, high) + times(groups_t, low)

    @pl.when(step < slots)
    def _():
        values = slot_ref[0, 0] - STEP_SIZE * grad
        me = lax.axis_index("pos")
        holder = slot_blocks_ref[me, step]
        listing = jnp.maximum(holder, 0)
        hit = partner_ref[listing, 0] == me
        for k in range(1, slots):
            hit = hit | (partner_ref[listing, k] == me)
        keep = jnp.where(hit & (holder >= 0), 1.0, 0.0).astype(F32)
        new_slots_ref[0, 0] = values * expand(factors(values) * keep)

    @pl.when(step == slots)
    def _():
        values = diag_ref[0] - STEP_SIZE * grad
        row = lax.broadcasted_iota(jnp.int32, (block_len, block_len), 0)
        column = lax.broadcasted_iota(jnp.int32, (block_len, block_len), 1)
        factor = jnp.where(row == column, 0.0, factors(values))
        new_diag_ref[0] = values * expand(factor)
        ones = jnp.ones((8, resid.shape[0]), BF16)
        new_fields_ref[...] = fields_ref[...] - STEP_SIZE * times(ones, resid)[:1]


def apply_step(slot_blocks, partner_blocks, gathered, states_all, fields, diag_couplings, slot_couplings):
    seqs, _, seq_rows, width = gathered.shape
    slots = slot_couplings.shape[1]
    block_len = states_all.shape[1]
    states_count = width // block_len
    last = slots - 1
    spec = pltpu.PrefetchScalarGridSpec(
        num_scalar_prefetch=2,
        grid=(slots + 1,),
        in_specs=[
            pl.BlockSpec((seqs, 1, seq_rows, width), lambda i, ids, alive: (0, i, 0, 0)),
            pl.BlockSpec(states_all.shape, lambda i, ids, alive: (0, 0, 0)),
            pl.BlockSpec((1, width), lambda i, ids, alive: (0, 0)),
            pl.BlockSpec((1, width, width), lambda i, ids, alive: (0, 0, 0)),
            pl.BlockSpec((1, 1, width, width), lambda i, ids, alive: (0, jnp.minimum(i, last), 0, 0)),
        ],
        out_specs=[
            pl.BlockSpec((1, width), lambda i, ids, alive: (0, 0)),
            pl.BlockSpec((1, width, width), lambda i, ids, alive: (0, 0, 0)),
            pl.BlockSpec((1, 1, width, width), lambda i, ids, alive: (0, jnp.minimum(i, last), 0, 0)),
        ],
        scratch_shapes=[pltpu.VMEM((seqs * seq_rows, width), BF16)],
    )
    new_fields, new_diag, new_slots = pl.pallas_call(
        functools.partial(step_kernel, block_len, states_count, slots),
        grid_spec=spec,
        out_shape=[
            jax.ShapeDtypeStruct((1, width), F32),
            jax.ShapeDtypeStruct(diag_couplings.shape, F32),
            jax.ShapeDtypeStruct(slot_couplings.shape, F32),
        ],
        compiler_params=pltpu.CompilerParams(vmem_limit_bytes=40 * 1024 * 1024),
    )(slot_blocks, partner_blocks, gathered, states_all, fields, diag_couplings, slot_couplings)
    return new_fields.reshape(block_len, states_count), new_diag, new_slots


def per_device(
    states, multiplicity, fields, diag_couplings, slot_couplings, slot_blocks, partner_blocks
):
    fields_row = fields.reshape(1, -1)
    gathered, states_all = exchange(
        slot_blocks,
        partner_blocks,
        states.T.astype(BF16),
        multiplicity.astype(F32)[:, None],
        fields_row,
        diag_couplings,
        slot_couplings,
    )
    return apply_step(
        slot_blocks, partner_blocks, gathered, states_all, fields_row, diag_couplings, slot_couplings
    )


def solution(mesh):
    placed = (
        P("seq", "pos"),
        P("seq"),
        P("pos", None),
        P("pos", None, None),
        P("pos", None, None, None),
        P(),
        P(),
    )
    return jax.shard_map(
        per_device,
        mesh=mesh,
        in_specs=placed,
        out_specs=(P("pos", None), P("pos", None, None), P("pos", None, None, None)),
        check_vma=False,
    )
```

```python
import functools
import jax
import jax.numpy as jnp
from jax import lax
from jax.experimental import pallas as pl
from jax.experimental.pallas import tpu as pltpu
from jax.sharding import PartitionSpec as P

STEP_SIZE = 0.2
THRESHOLD = 0.3
F32 = jnp.float32
BF16 = jnp.bfloat16


def halves(values):
    high = values.astype(BF16)
    return high, (values - high.astype(F32)).astype(BF16)


def times(left, right):
    return jnp.dot(left, right, preferred_element_type=F32)


def indicator(rows, columns, states_count):
    row = lax.broadcasted_iota(jnp.int32, (rows, columns), 0)
    column = lax.broadcasted_iota(jnp.int32, (rows, columns), 1)
    return jnp.where((column >= row * states_count) & (column < (row + 1) * states_count), 1.0, 0.0).astype(BF16)


def indicator_t(rows, columns, states_count):
    row = lax.broadcasted_iota(jnp.int32, (rows, columns), 0)
    column = lax.broadcasted_iota(jnp.int32, (rows, columns), 1)
    return jnp.where((row >= column * states_count) & (row < (column + 1) * states_count), 1.0, 0.0).astype(BF16)


def position_starts(block_len, states_count):
    column = lax.broadcasted_iota(jnp.int32, (1, block_len * states_count), 1)
    start = jnp.zeros_like(column)
    for p in range(1, block_len):
        start = jnp.where(column >= p * states_count, p * states_count, start)
    return column, start


def row_of(fields, groups, column, start):
    block_len, states_count = fields.shape
    state = lax.broadcasted_iota(jnp.int32, (states_count, column.shape[1]), 0)
    spread = jnp.where(state == column - start, 1.0, 0.0).astype(BF16)
    first = fields.astype(BF16)
    rest = fields - first.astype(F32)
    second, third = halves(rest)
    wide = times(third, spread) + times(second, spread) + times(first, spread)
    return jnp.sum(wide * groups.astype(F32), axis=0, keepdims=True)


def onehot_of(states_t, groups, column, start):
    spread = lax.dot_general(
        states_t, groups, (((0,), (0,)), ((), ())), preferred_element_type=F32
    )
    return jnp.where(spread == (column - start).astype(F32), 1.0, 0.0).astype(BF16)


def exchange_kernel(
    block_len, states_count, seqs, highs, lows,
    slot_blocks_ref, partner_ref, states_ref, multiplicity_ref, fields_ref, diag_ref, slot_ref,
    out_ref, states_out_ref,
    term_ref, near_ref, high1_ref, stage1_ref, low1_ref, high2_ref, stage2_ref, low2_ref,
    logits_ref, send_sem, recv_sem,
):
    width = block_len * states_count
    slots = slot_ref.shape[1]
    far = slots - 2
    blocks = highs * lows
    seq = lax.axis_index("seq")
    pos = lax.axis_index("pos")
    high = pos // lows
    low = pos % lows

    def place(f, target):
        return (lax.rem(seq + f, seqs), target)

    def beside(g):
        return lax.rem(pos + g + blocks, blocks)

    def high_peer(d):
        return lax.rem(high + d, highs) * lows + low

    def low_peer(e):
        return high * lows + lax.rem(low + e, lows)

    near = [(f, g) for g in (0, 1, -1) for f in range(seqs) if (f, g) != (0, 0)]
    peers = [place(f, beside(g)) for f, g in near]
    peers += [place(0, high_peer(d)) for d in range(1, highs)]
    peers += [place(0, low_peer(e)) for e in range(1, lows)]
    barrier = pltpu.get_barrier_semaphore()
    for peer in peers:
        pl.semaphore_signal(barrier, inc=1, device_id=peer, device_id_type=pl.DeviceIdType.MESH)

    groups = indicator(block_len, width, states_count)
    column, start = position_starts(block_len, states_count)
    onehot = onehot_of(states_ref[...], groups, column, start)

    def terms(values):
        first = values.astype(BF16)
        rest = values - first.astype(F32)
        second = rest.astype(BF16)
        third = (rest - second.astype(F32)).astype(BF16)
        total = None
        for part in (third, second, first):
            product = lax.dot_general(
                onehot, part, (((1,), (1,)), ((), ())), preferred_element_type=F32
            )
            total = product if total is None else total + product
        return total

    copies = []

    def send(source, target, device):
        k = len(copies)
        copy = pltpu.make_async_remote_copy(
            src_ref=source, dst_ref=target, send_sem=send_sem.at[k], recv_sem=recv_sem.at[k],
            device_id=device, device_id_type=pl.DeviceIdType.MESH,
        )
        copy.start()
        copies.append(copy)
        return copy

    rows = states_ref.shape[1]
    chunks = len(high1_ref)
    depth = rows // chunks
    parts = [pl.ds(r * depth, depth) for r in range(chunks)]

    for t in range(far):
        value = terms(slot_ref[0, 2 + t]).astype(BF16)
        for r in range(chunks):
            high1_ref[r][0, t] = value[r * depth : (r + 1) * depth]
    states_out_ref[0] = states_ref[...]
    pl.semaphore_wait(barrier, len(peers))
    high1 = [
        [
            send(high1_ref[r].at[0], high1_ref[r].at[d], place(0, high_peer(d)))
            for d in range(1, highs)
        ]
        for r in range(chunks)
    ]
    for t in range(2):
        term_ref[t] = terms(slot_ref[0, t]).astype(BF16)
    near1 = [
        send(term_ref.at[0], near_ref.at[0], place(0, beside(-1))),
        send(term_ref.at[1], near_ref.at[1], place(0, beside(1))),
    ]
    states_moves = [
        send(states_ref, states_out_ref.at[f], place(f, pos)) for f in range(1, seqs)
    ]
    mask = jnp.zeros((width, width), jnp.bool_)
    row = lax.broadcasted_iota(jnp.int32, (width, width), 0)
    wide = lax.broadcasted_iota(jnp.int32, (width, width), 1)
    for p in range(block_len):
        lo, hi = p * states_count, (p + 1) * states_count
        mask = mask | ((row >= lo) & (row < hi) & (wide >= lo) & (wide < hi))
    logits_ref[...] = row_of(fields_ref[...], groups, column, start) + terms(jnp.where(mask, 0.0, diag_ref[0]))
    same = jnp.where(mask, 1.0, 0.0).astype(BF16)

    def search(target, t):
        def one(c, found):
            return jnp.where(slot_blocks_ref[c, t] == target, c, found)

        return lax.fori_loop(0, blocks, one, jnp.int32(-1))

    def listed(holder):
        hit = partner_ref[pos, 0] == holder
        for k in range(1, slots):
            hit = hit | (partner_ref[pos, k] == holder)
        return jnp.where(hit & (holder >= 0), 1.0, 0.0).astype(F32)

    def ring(value, size):
        return lax.rem(value + size, size)

    holders = [search(pos, t) for t in range(slots)]
    alive = [listed(holder) for holder in holders]
    order = list(range(1, lows)) + [0]
    picks1, picks2 = {}, {}
    for e in order:
        target = low_peer(e)
        for t in range(far):
            pick = jnp.int32(0)
            for h in range(highs):
                found = slot_blocks_ref[h * lows + low, 2 + t] == target
                pick = jnp.where(found, ring(high - h, highs), pick)
            picks1[e, t] = pick
            wanted = jnp.maximum(slot_blocks_ref[target, 2 + t], 0)
            picks2[e, t] = ring(high - wanted // lows, highs)
    across = lax.broadcasted_iota(jnp.int32, (rows, rows), 0)
    along = lax.broadcasted_iota(jnp.int32, (rows, rows), 1)
    counts = jnp.where(across == along, multiplicity_ref[...], 0).astype(F32)
    weight = 1.0 / jnp.sum(counts, axis=1, keepdims=True)

    def pass_low(load, stage_ref, low_ref):
        sent = []
        for e in order:
            for t in range(far):
                value = load(e, t)
                if e == 0:
                    low_ref[0, t] = value
                else:
                    stage_ref[e, t] = value
            if e:
                sent.append(
                    send(
                        stage_ref.at[e],
                        low_ref.at[e],
                        place(0, low_peer(e)),
                    )
                )
        return sent

    low1 = []
    for r in range(chunks):
        for copy in high1[r]:
            copy.wait_recv()
        low1.append(
            pass_low(lambda e, t: high1_ref[r][picks1[e, t], t], stage1_ref[r], low1_ref[r])
        )
    for copy in near1:
        copy.wait_recv()
    slot_of = {0: slots, 1: 0, -1: 1}
    high2, last = [], []
    column_start = start
    for r, part in enumerate(parts):
        logits = logits_ref[part] + near_ref[0, part].astype(F32) * alive[0]
        logits += near_ref[1, part].astype(F32) * alive[1]
        for copy in low1[r]:
            copy.wait_recv()
        for t in range(far):
            holder = jnp.maximum(holders[2 + t], 0)
            pick = ring(low - lax.rem(holder, lows), lows)
            logits += low1_ref[r][pick, t].astype(F32) * alive[2 + t]
        peak = jnp.zeros_like(logits)
        for p in range(block_len):
            inside = column_start == p * states_count
            top = jnp.max(jnp.where(inside, logits, -jnp.inf), axis=1, keepdims=True)
            peak = jnp.where(inside, top, peak)
        powers = jnp.exp(logits - peak)
        first, second = halves(powers)
        probabilities = powers / (times(first, same) + times(second, same))
        mine = slice(r * depth, (r + 1) * depth)
        residual = (weight[mine] * (probabilities - onehot[mine].astype(F32))).astype(BF16)
        high2_ref[r][0] = residual
        out_ref[0, slots, part] = residual
        high2.append(
            [
                send(high2_ref[r].at[0], high2_ref[r].at[d], place(0, high_peer(d)))
                for d in range(1, highs)
            ]
        )
        last += [
            send(high2_ref[r].at[0], out_ref.at[f, slot_of[g], part], place(f, beside(g)))
            for f, g in near
        ]
    low2 = []
    for r in range(chunks):
        for copy in high2[r]:
            copy.wait_recv()
        low2.append(
            pass_low(lambda e, t: high2_ref[r][picks2[e, t]], stage2_ref[r], low2_ref[r])
        )
    ends = pl.ds(2, far)
    for r, part in enumerate(parts):
        for copy in low2[r]:
            copy.wait_recv()
        for t in range(far):
            wanted = jnp.maximum(slot_blocks_ref[pos, 2 + t], 0)
            pick = ring(low - lax.rem(wanted, lows), lows)
            out_ref[0, 2 + t, part] = low2_ref[r][pick, t]
        last += [
            send(out_ref.at[0, ends, part], out_ref.at[f, ends, part], place(f, pos))
            for f in range(1, seqs)
        ]
    for copy in states_moves + last:
        copy.wait_recv()
    for copy in copies:
        copy.wait_send()


def exchange(slot_blocks, partner_blocks, states_t, multiplicity, fields, diag, slot):
    block_len, seq_rows = states_t.shape
    width = fields.size
    slots = slot.shape[1]
    seqs, blocks = lax.axis_size("seq"), lax.axis_size("pos")
    lows = 4 if blocks % 4 == 0 else 1
    highs = blocks // lows
    vmem = pl.BlockSpec(memory_space=pltpu.VMEM)
    smem = pl.BlockSpec(memory_space=pltpu.SMEM)
    far = slots - 2
    tile = (seq_rows, width)
    chunks = 4 if seq_rows % 64 == 0 else 1
    moves = 2 * chunks * (highs + lows) + (4 * chunks + 1) * seqs
    piece = (seq_rows // chunks, width)
    return pl.pallas_call(
        functools.partial(exchange_kernel, block_len, width // block_len, seqs, highs, lows),
        in_specs=[smem, smem, vmem, vmem, vmem, vmem, vmem],
        out_specs=[vmem, vmem],
        out_shape=[
            jax.ShapeDtypeStruct((seqs, slots + 1) + tile, BF16),
            jax.ShapeDtypeStruct((seqs, block_len, seq_rows), BF16),
        ],
        scratch_shapes=[
            pltpu.VMEM((2,) + tile, BF16),
            pltpu.VMEM((2,) + tile, BF16),
            [pltpu.VMEM((highs, far) + piece, BF16)] * chunks,
            [pltpu.VMEM((lows, far) + piece, BF16)] * chunks,
            [pltpu.VMEM((lows, far) + piece, BF16)] * chunks,
            [pltpu.VMEM((highs,) + piece, BF16)] * chunks,
            [pltpu.VMEM((lows, far) + piece, BF16)] * chunks,
            [pltpu.VMEM((lows, far) + piece, BF16)] * chunks,
            pltpu.VMEM(tile, F32),
            pltpu.SemaphoreType.DMA((moves,)),
            pltpu.SemaphoreType.DMA((moves,)),
        ],
        compiler_params=pltpu.CompilerParams(
            collective_id=0, has_side_effects=True, vmem_limit_bytes=48 * 1024 * 1024
        ),
    )(slot_blocks, partner_blocks, states_t, multiplicity, fields, diag, slot)


def step_kernel(
    block_len, states_count, slots,
    slot_blocks_ref, partner_ref, resid_ref, states_ref, fields_ref, diag_ref, slot_ref,
    new_fields_ref, new_diag_ref, new_slots_ref, onehot_ref,
):
    width = block_len * states_count
    step = pl.program_id(0)
    groups = indicator(block_len, width, states_count)
    groups_t = indicator_t(width, block_len, states_count)

    @pl.when(step == 0)
    def _():
        column, start = position_starts(block_len, states_count)
        seq_rows = states_ref.shape[2]
        for f in range(states_ref.shape[0]):
            onehot_ref[pl.ds(f * seq_rows, seq_rows)] = onehot_of(
                states_ref[f], groups, column, start
            )

    resid = resid_ref[...].reshape(-1, width)
    grad = lax.dot_general(
        resid, onehot_ref[...], (((0,), (0,)), ((), ())), preferred_element_type=F32
    )

    def factors(values):
        high, low = halves(values * values)
        sums = times(groups, high) + times(groups, low)
        high, low = halves(sums)
        sums = times(high, groups_t) + times(low, groups_t)
        factor = jnp.maximum(0.0, 1.0 - THRESHOLD / jnp.sqrt(sums + 1e-06))
        return factor

    def expand(factor):
        high, low = halves(factor)
        wide = times(high, groups) + times(low, groups)
        high, low = halves(wide)
        return times(groups_t, high) + times(groups_t, low)

    @pl.when(step < slots)
    def _():
        values = slot_ref[0, 0] - STEP_SIZE * grad
        me = lax.axis_index("pos")
        holder = slot_blocks_ref[me, step]
        listing = jnp.maximum(holder, 0)
        hit = partner_ref[listing, 0] == me
        for k in range(1, slots):
            hit = hit | (partner_ref[listing, k] == me)
        keep = jnp.where(hit & (holder >= 0), 1.0, 0.0).astype(F32)
        new_slots_ref[0, 0] = values * expand(factors(values) * keep)

    @pl.when(step == slots)
    def _():
        values = diag_ref[0] - STEP_SIZE * grad
        row = lax.broadcasted_iota(jnp.int32, (block_len, block_len), 0)
        column = lax.broadcasted_iota(jnp.int32, (block_len, block_len), 1)
        factor = jnp.where(row == column, 0.0, factors(values))
        new_diag_ref[0] = values * expand(factor)
        ones = jnp.ones((8, resid.shape[0]), BF16)
        new_fields_ref[...] = row_of(fields_ref[...], groups, *position_starts(block_len, states_count)) - STEP_SIZE * times(ones, resid)[:1]


def apply_step(slot_blocks, partner_blocks, gathered, states_all, fields, diag_couplings, slot_couplings):
    seqs, _, seq_rows, width = gathered.shape
    slots = slot_couplings.shape[1]
    block_len = states_all.shape[1]
    states_count = width // block_len
    last = slots - 1
    spec = pltpu.PrefetchScalarGridSpec(
        num_scalar_prefetch=2,
        grid=(slots + 1,),
        in_specs=[
            pl.BlockSpec((seqs, 1, seq_rows, width), lambda i, ids, alive: (0, i, 0, 0)),
            pl.BlockSpec(states_all.shape, lambda i, ids, alive: (0, 0, 0)),
            pl.BlockSpec(fields.shape, lambda i, ids, alive: (0, 0)),
            pl.BlockSpec((1, width, width), lambda i, ids, alive: (0, 0, 0)),
            pl.BlockSpec((1, 1, width, width), lambda i, ids, alive: (0, jnp.minimum(i, last), 0, 0)),
        ],
        out_specs=[
            pl.BlockSpec((1, width), lambda i, ids, alive: (0, 0)),
            pl.BlockSpec((1, width, width), lambda i, ids, alive: (0, 0, 0)),
            pl.BlockSpec((1, 1, width, width), lambda i, ids, alive: (0, jnp.minimum(i, last), 0, 0)),
        ],
        scratch_shapes=[pltpu.VMEM((seqs * seq_rows, width), BF16)],
    )
    new_fields, new_diag, new_slots = pl.pallas_call(
        functools.partial(step_kernel, block_len, states_count, slots),
        grid_spec=spec,
        out_shape=[
            jax.ShapeDtypeStruct((1, width), F32),
            jax.ShapeDtypeStruct(diag_couplings.shape, F32),
            jax.ShapeDtypeStruct(slot_couplings.shape, F32),
        ],
        compiler_params=pltpu.CompilerParams(vmem_limit_bytes=40 * 1024 * 1024),
    )(slot_blocks, partner_blocks, gathered, states_all, fields, diag_couplings, slot_couplings)
    return new_fields.reshape(block_len, states_count), new_diag, new_slots


def per_device(
    states, multiplicity, fields, diag_couplings, slot_couplings, slot_blocks, partner_blocks
):
    gathered, states_all = exchange(
        slot_blocks,
        partner_blocks,
        states.T.astype(BF16),
        multiplicity[None, :],
        fields,
        diag_couplings,
        slot_couplings,
    )
    return apply_step(
        slot_blocks, partner_blocks, gathered, states_all, fields, diag_couplings, slot_couplings
    )


def solution(mesh):
    placed = (
        P("seq", "pos"),
        P("seq"),
        P("pos", None),
        P("pos", None, None),
        P("pos", None, None, None),
        P(),
        P(),
    )
    return jax.shard_map(
        per_device,
        mesh=mesh,
        in_specs=placed,
        out_specs=(P("pos", None), P("pos", None, None), P("pos", None, None, None)),
        check_vma=False,
    )
```
